32 devices in a mesh: grp: 4 (over y, x), mem: 8 (over z, core).
Axes of the slice: x: 2, y: 2, z: 4, core: 2. Of those that a mesh axis runs over, the one named last changes fastest.
Arguments:
- solution: bfloat16 [7, 7, 7, 32, 16, 256], P(None, None, None, 'mem', 'grp'), may hold values from -1.5 to 1.5
- source: bfloat16 [7, 7, 7, 32, 16, 256], P(None, None, None, 'mem', 'grp'), may hold values from -6 to 6
- degree: int32 [32, 16, 256], P('mem', 'grp'), may hold values from 2 to 6
Outputs:
- updated: float32 [7, 7, 7, 32, 16, 256], P(None, None, None, 'mem', 'grp')
- fine_residual: bfloat16 [7, 7, 7, 32, 16, 256], P(None, None, None, 'mem', 'grp')
The draws below stay inside these ranges and needn't reach their ends.
All inputs are finite; a program needn't handle non-finite values.
Results may differ from the reference program's by a relative error of at most 0.0049.
Values may be sent and summed in bfloat16 or wider, within the bound.
A program may use at most 128 MiB of HBM per device.

```python
import math
import jax
import jax.numpy as jnp
from jax import lax

MODES = 7
EZ = 256
NX = 32
NY = 16


def set_ends(drawn, rng, low, largest):
    index_at = [jax.random.randint(jax.random.fold_in(rng, axis), (), 0, length) for axis, length in enumerate(drawn.shape)]
    main_axis = drawn.shape.index(max(drawn.shape))
    beside = index_at[:main_axis] + [(index_at[main_axis] + 1) % drawn.shape[main_axis]] + index_at[main_axis + 1:]
    return drawn.at[tuple(index_at)].set(low).at[tuple(beside)].set(largest)


def shard_levels(key, shape, cuts, smallest, high):
    loudness, own = 1.0, jax.random.fold_in(key, 6)
    for dim, parts in cuts:
        draws = jnp.exp(jax.random.uniform(jax.random.fold_in(own, dim), (parts,), jnp.float32, smallest / len(cuts), high / len(cuts)))
        loudness = loudness * jnp.repeat(draws, shape[dim] // parts).reshape([-1 if axis == dim else 1 for axis in range(len(shape))])
    return loudness


def scatter_about(stream_key, shape, scale, bound, split=(), kind=jnp.bfloat16):
    array = scale * jax.random.normal(stream_key, shape, jnp.float32)
    if split:
        array = array * shard_levels(stream_key, shape, split, -0.22, 0.18)
    return jnp.clip(array, -bound, bound).astype(kind)


def setup_inputs(seed: int = 0) -> dict:
    arg_keys = jax.random.split(jax.random.key(seed), 4)
    solution = scatter_about(arg_keys[0], (MODES, MODES, MODES, NX, NY, EZ), 0.1, 1.5, ((3, 8), (4, 4)))
    source = scatter_about(arg_keys[1], (MODES, MODES, MODES, NX, NY, EZ), 1.0, 6.0, ((3, 8), (4, 4)))
    degree = set_ends(jax.random.randint(arg_keys[2], (NX, NY, EZ), 2, 7), jax.random.fold_in(arg_keys[2], 1), 2, 6).astype(jnp.int32)
    return {"solution": solution, "source": source, "degree": degree}


PENALTY = 3.0
OMEGA = 0.5
SCALING = 0.00390625
HIGH = lax.Precision.HIGHEST

def legendre_tables(length):
    scales = [math.sqrt((2.0 * i + 1.0) / 2.0) for i in range(length)]
    alternate = [1.0 if i % 2 == 0 else -1.0 for i in range(length)]
    slopes = [i * (i + 1.0) / 2.0 for i in range(length)]
    right = [scales[i] for i in range(length)]
    left = [scales[i] * alternate[i] for i in range(length)]
    right_slope = [scales[i] * slopes[i] for i in range(length)]
    left_slope = [-scales[i] * alternate[i] * slopes[i] for i in range(length)]
    stiffness = []
    for i in range(length):
        line = []
        for j in range(length):
            lesser = float(min(i, j))
            parity = 1.0 if (i + j) % 2 == 0 else 0.0
            line.append(math.sqrt((2.0 * i + 1.0) * (2.0 * j + 1.0)) / 2.0 * lesser * (lesser + 1.0) * parity)
        stiffness.append(line)
    listed = (right, left, right_slope, left_slope, stiffness)
    return tuple((jnp.asarray(matrix, dtype=jnp.float32) for matrix in listed))

def product(table, field, table_axis, direction):
    if field.dtype == jnp.bfloat16:
        return jnp.tensordot(table, field, axes=([table_axis], [direction]), preferred_element_type=jnp.float32)
    return jnp.tensordot(table, field, axes=([table_axis], [direction]), precision=HIGH)

def contract(field, table, direction):
    return product(table, field, 0, direction)

def lifted(face_flux, table, direction):
    broadcast_shape = [1] * (face_flux.ndim + 1)
    broadcast_shape[direction] = table.shape[0]
    return jnp.expand_dims(face_flux, direction) * table.reshape(broadcast_shape).astype(jnp.float32)

def operate(field, penalty, tables, neighbours):
    right, left, right_slope, left_slope, stiffness = tables
    result = jnp.zeros(field.shape, jnp.float32)
    for direction in range(3):
        result = result + jnp.moveaxis(product(stiffness, field, 1, direction), 0, direction)
    for direction in range(3):
        right_value = contract(field, right, direction)
        right_deriv = contract(field, right_slope, direction)
        left_value = contract(field, left, direction)
        left_deriv = contract(field, left_slope, direction)
        if direction == 0:
            prev_value, prev_deriv, prev_pen, next_value, next_deriv, next_pen = neighbours(right_value, right_deriv, left_value, left_deriv)
        else:
            space_dim = direction + 2
            prev_value = jnp.roll(right_value, 1, space_dim)
            prev_deriv = jnp.roll(right_deriv, 1, space_dim)
            prev_pen = jnp.roll(penalty, 1, space_dim)
            next_value = jnp.roll(left_value, -1, space_dim)
            next_deriv = jnp.roll(left_deriv, -1, space_dim)
            next_pen = jnp.roll(penalty, -1, space_dim)
        jump_up = right_value - next_value
        flux_up = jnp.maximum(penalty, next_pen) * jump_up - 0.5 * (right_deriv + next_deriv)
        jump_down = prev_value - left_value
        flux_down = jnp.maximum(prev_pen, penalty) * jump_down - 0.5 * (prev_deriv + left_deriv)
        result = result + lifted(flux_up, right, direction) - 0.5 * lifted(jump_up, right_slope, direction)
        result = result - lifted(flux_down, left, direction) - 0.5 * lifted(jump_down, left_slope, direction)
    return SCALING * result

def shift_down(values):
    return jnp.concatenate([jnp.zeros_like(values[:, :, :1]), values[:, :, :-1]], axis=2)

def shift_up(values):
    return jnp.concatenate([values[:, :, 1:], jnp.zeros_like(values[:, :, :1])], axis=2)

def zero_neighbours(penalty):

    def neighbours(right_value, right_deriv, left_value, left_deriv):
        return (shift_down(right_value), shift_down(right_deriv), shift_down(penalty), shift_up(left_value), shift_up(left_deriv), shift_up(penalty))
    return neighbours

def coarse_diagonal(tables):
    right, left, right_slope, left_slope, stiffness = tables
    single = jnp.diagonal(stiffness) + 2.0 * (4.0 * PENALTY * right * right - right * right_slope)
    total = single[:, None, None] + single[None, :, None] + single[None, None, :]
    return SCALING * total.reshape(2, 2, 2, 1, 1, 1)

def reference(solution, source, degree):
    length = solution.shape[0]
    tables = legendre_tables(length)
    fine_tables = tuple((matrix.astype(jnp.bfloat16) for matrix in tables))
    coarse_tables = tuple((matrix[:2] for matrix in tables[:4])) + (tables[4][:2, :2],)
    index_range = jnp.arange(length, dtype=jnp.int32)
    levels = jnp.maximum(jnp.maximum(index_range[:, None, None], index_range[None, :, None]), index_range[None, None, :])
    inside = levels[:, :, :, None, None, None] <= degree[None, None, None]
    mask = inside.astype(jnp.float32)
    start = jnp.where(inside, solution, jnp.zeros_like(solution))
    penalty = (PENALTY * ((degree + 1) * (degree + 1)).astype(jnp.float32))[None, None]
    residual_full = mask * (source.astype(jnp.float32) - operate(start, penalty, fine_tables, zero_neighbours(penalty)))
    coarse = residual_full[:2, :2, :2]
    diagonal = coarse_diagonal(coarse_tables)
    coarse_pen = jnp.full((1, 1) + coarse.shape[3:], 4.0 * PENALTY, jnp.float32)
    first = OMEGA * coarse / diagonal
    second = first + OMEGA * (coarse - operate(first, coarse_pen, coarse_tables, zero_neighbours(coarse_pen))) / diagonal
    padding = ((0, length - 2),) * 3 + ((0, 0),) * 3
    updated = start.astype(jnp.float32) + jnp.pad(second, padding)
    return (updated, residual_full.astype(jnp.bfloat16))
```

```python
import functools
import math

import jax
import jax.numpy as jnp
import numpy as np
from jax import lax
from jax.experimental import pallas as pl
from jax.experimental.pallas import tpu as pltpu
from jax.sharding import PartitionSpec as P

BF = jnp.bfloat16
F32 = jnp.float32
SCALING = 0.00390625
MESH = pl.DeviceIdType.MESH


def tables(n):
    i = np.arange(n)
    w = np.sqrt((2.0 * i + 1.0) / 2.0)
    alt = np.where(i % 2 == 0, 1.0, -1.0)
    s = i * (i + 1.0) / 2.0
    low = np.minimum(i[:, None], i[None, :]).astype(np.float64)
    even = (i[:, None] + i[None, :]) % 2 == 0
    k = np.sqrt((2.0 * i[:, None] + 1.0) * (2.0 * i[None, :] + 1.0)) / 2.0 * low * (low + 1.0) * even
    listed = (w, w * alt, w * s, -w * alt * s, k)
    return [t.astype(np.float32).astype(BF).astype(np.float64) for t in listed]


def place(lx, ly, direction):
    e = np.arange(lx * ly)
    x, y = e // ly, e % ly
    if direction == 0:
        return x, lx, ly, y
    return y, ly, 1, x


def matrices(n, lx, ly):
    right, left, rs, ls, k = tables(n)
    el = lx * ly
    eye = np.eye(el)
    out = {}
    for d in range(2):
        c, count, stride, other = place(lx, ly, d)
        g = el // count
        up = np.zeros((el, el))
        dn = np.zeros((el, el))
        hi = np.zeros((el, g))
        lo = np.zeros((el, g))
        for e in range(el):
            if c[e] < count - 1:
                up[e, e + stride] = 1.0
            else:
                hi[e, other[e]] = 1.0
            if c[e] > 0:
                dn[e, e - stride] = 1.0
            else:
                lo[e, other[e]] = 1.0
        z = np.zeros((el, g))
        for par in range(2):
            def slab(a, b, par=par):
                pad = np.zeros((el, 2 * g))
                both = np.concatenate([a, b], axis=1)
                return np.concatenate([both, pad] if par == 0 else [pad, both], axis=1)

            none = slab(z, z)
            rows = [
                [np.kron(right, eye) - np.kron(left, up), none, slab(-hi, z)],
                [0.5 * (np.kron(rs, eye) + np.kron(ls, up)), none, slab(z, 0.5 * hi)],
                [np.kron(right, dn) - np.kron(left, eye), slab(lo, z), none],
                [0.5 * (np.kron(rs, dn) + np.kron(ls, eye)), slab(z, 0.5 * lo), none],
            ]
            out[f"t{d}{par}"] = np.block(rows)
            q = np.zeros((el, el))
            rows = [
                [up, up, q, q, q, q, none, slab(hi, z)],
                [q, q, q, q, up, up, none, slab(z, hi)],
                [q, q, dn, dn, q, q, slab(lo, z), none],
                [q, q, q, q, dn, dn, slab(z, lo), none],
            ]
            out[f"s{d}{par}"] = np.block(rows)
        eh, elow = hi.T, lo.T
        zz = np.zeros((2 * g, n * el))
        u = np.concatenate([np.kron(right, eh), np.kron(rs, eh)])
        v = np.concatenate([np.kron(left, elow), np.kron(ls, elow)])
        out[f"e{d}"] = np.block([[u, zz], [zz, u], [v, zz], [zz, v]])
        zp = np.zeros((2 * g, el))
        ph = np.concatenate([eh, np.zeros((g, el))])
        plo = np.concatenate([elow, np.zeros((g, el))])
        out[f"f{d}"] = np.block([[u, zp], [zz, ph], [v, zp], [zz, plo]])
        qz = np.zeros((el, 2 * g))
        none = np.zeros((el, 4 * g))
        out[f"q{d}"] = np.block(
            [
                [up, none, np.concatenate([qz, hi, z], axis=1)],
                [dn, np.concatenate([qz, lo, z], axis=1), none],
            ]
        )
        o = np.zeros((g, el))
        cu = np.block([[o, o, eh, eh, o, o], [o, o, o, o, eh, eh]])
        cd = np.block([[elow, elow, o, o, o, o], [o, o, o, o, elow, elow]])
        cz = np.zeros_like(cu)
        out[f"c{d}"] = np.block([[cu, cz], [cz, cu], [cd, cz], [cz, cd]])
    out["tz"] = np.concatenate(
        [np.kron(right, eye), np.kron(0.5 * rs, eye), np.kron(left, eye), np.kron(0.5 * ls, eye)]
    )
    ju = -0.5 * np.kron(rs[:, None], eye)
    fu = np.kron(right[:, None], eye)
    jd = -0.5 * np.kron(ls[:, None], eye)
    fd = -np.kron(left[:, None], eye)
    out["w"] = -SCALING * np.concatenate(
        [np.kron(k, eye), ju, ju, fu, fu, jd, jd, fd, fd], axis=1
    )
    return {name: m.astype(np.float32).astype(BF) for name, m in out.items()}


def dot(a, b):
    return jnp.dot(a, b, preferred_element_type=F32)


def split(v):
    hi = v.astype(BF)
    return [hi, (v - hi.astype(F32)).astype(BF)]


def roll(v, shift):
    return pltpu.roll(v, shift % v.shape[1], 1)


def rows_of(n, d, p):
    if d == 0:
        return p, n * n
    if d == 1:
        return (p // n) * (n * n) + p % n, n
    return p * n, 1


def gather(f_ref, n, d, p):
    base, step = rows_of(n, d, p)
    return [f_ref[base + step * i] for i in range(n)]


def pair_update(n, d, field, ghosts, tmat, w, pens):
    el = field[0].shape[0]
    if d < 2:
        t = dot(tmat, jnp.concatenate(field + ghosts, axis=0))
        ju, mu, jd, md = (t[a * el : (a + 1) * el] for a in range(4))
        fu = pens[0] * ju - mu
        fd = pens[1] * jd - md
    else:
        t = dot(tmat, jnp.concatenate(field, axis=0))
        tr, gr, tl, gl = (t[a * el : (a + 1) * el] for a in range(4))
        ju = tr - roll(tl, -1)
        fu = pens[0] * ju - (gr + roll(gl, -1))
        jd = roll(ju, 1)
        fd = roll(fu, 1)
    return dot(w, jnp.concatenate(field + split(ju) + split(fu) + split(jd) + split(fd), axis=0))


def exchange_kernel(n, names, scale, sol, deg, srcc, *refs):
    count = len(names)
    mats = dict(zip(names, refs[:count]))
    (f_ref, g0lo, g0hi, g1lo, g1hi, pens, second, s_up0, s_dn0, s_up1, s_dn1, r_lo0, r_hi0, r_lo1,
     r_hi1, cs_up0, cs_dn0, cs_up1, cs_dn1, cr_lo0, cr_hi0, cr_lo1, cr_hi1, send, recv) = refs[count:]
    mem, grp = lax.axis_index("mem"), lax.axis_index("grp")
    nmem, ngrp = lax.axis_size("mem"), lax.axis_size("grp")
    below = {"grp": grp, "mem": jnp.maximum(mem - 1, 0)}
    above = {"grp": grp, "mem": jnp.minimum(mem + 1, nmem - 1)}
    south = {"grp": lax.rem(grp + ngrp - 1, ngrp), "mem": mem}
    north = {"grp": lax.rem(grp + 1, ngrp), "mem": mem}
    has_lo, has_hi = mem > 0, mem < nmem - 1
    lx, ly = sol.shape[1], sol.shape[2]
    el = lx * ly

    barrier = pltpu.get_barrier_semaphore()

    @pl.when(has_lo)
    def _():
        pl.semaphore_signal(barrier, inc=1, device_id=below, device_id_type=MESH)

    @pl.when(has_hi)
    def _():
        pl.semaphore_signal(barrier, inc=1, device_id=above, device_id_type=MESH)

    pl.semaphore_signal(barrier, inc=1, device_id=south, device_id_type=MESH)
    pl.semaphore_signal(barrier, inc=1, device_id=north, device_id_type=MESH)

    degree = deg[...]
    masks = [None] * 3 + [jnp.where(degree >= lv, 1.0, 0.0).astype(BF) for lv in range(3, n)]

    def build(i, carry):
        for j in range(n):
            for k in range(n):
                m = i * (n * n) + j * n + k
                v = jnp.concatenate([sol[m, x] for x in range(lx)], axis=0)
                mask_ref_level = max(j, k)
                f_ref[m] = v * mask_level(i, mask_ref_level)
        return carry

    def mask_level(i, lv):
        if isinstance(i, int):
            top = max(i, lv)
            return masks[top] if top > 2 else jnp.ones_like(masks[3])
        raise NotImplementedError

    for i in range(n):
        build(i, 0)

    pen = (3 * (degree + 1) * (degree + 1)).astype(F32)
    pen_b = pen.astype(BF)

    def edges(d, up, dn):
        e = mats[f"e{d}"][...]

        def body(q, carry):
            t = dot(e, jnp.concatenate(gather(f_ref, n, d, 2 * q) + gather(f_ref, n, d, 2 * q + 1), axis=0))
            up[q] = t[:el].astype(BF)
            dn[q] = t[el:].astype(BF)
            return carry

        half = (n * n) // 2
        lax.fori_loop(0, half, body, 0, unroll=4)
        t = dot(mats[f"f{d}"][...], jnp.concatenate(gather(f_ref, n, d, n * n - 1) + [pen_b], axis=0))
        up[half] = t[:el].astype(BF)
        dn[half] = t[el:].astype(BF)

    def copies(base, up0, dn0, up1, dn1, lo0, hi0, lo1, hi1):
        def mk(src, dst, k, to):
            return pltpu.make_async_remote_copy(
                src_ref=src, dst_ref=dst, send_sem=send.at[base + k], recv_sem=recv.at[base + k],
                device_id=to, device_id_type=MESH,
            )

        return (mk(up1, lo1, 2, north), mk(dn1, hi1, 3, south), mk(up0, lo0, 0, above), mk(dn0, hi0, 1, below))

    def start_y(c):
        c[0].start()
        c[1].start()

    def start_x(c, lo, hi):
        @pl.when(has_hi)
        def _():
            c[2].start()

        @pl.when(has_lo)
        def _():
            c[3].start()

        @pl.when(jnp.logical_not(has_lo))
        def _():
            lo[...] = jnp.zeros_like(lo)

        @pl.when(jnp.logical_not(has_hi))
        def _():
            hi[...] = jnp.zeros_like(hi)

    def finish(c):
        c[0].wait()
        c[1].wait()

        @pl.when(has_hi)
        def _():
            c[2].wait_send()
            c[3].wait_recv()

        @pl.when(has_lo)
        def _():
            c[3].wait_send()
            c[2].wait_recv()

    fine = copies(0, s_up0, s_dn0, s_up1, s_dn1, r_lo0, r_hi0, r_lo1, r_hi1)
    edges(1, s_up1, s_dn1)
    pl.semaphore_wait(barrier, 2 + has_lo.astype(jnp.int32) + has_hi.astype(jnp.int32))
    start_y(fine)
    edges(0, s_up0, s_dn0)
    start_x(fine, r_lo0, r_hi0)

    w_low = mats["w"][: 2 * el]
    zpen = jnp.maximum(pen, roll(pen, -1))
    pens[4] = zpen
    pens[5] = zpen
    coarse = [srcc[m].astype(F32) for m in range(8)]

    def add(d, c, t):
        a, b = c // 2, c % 2
        for i in range(2):
            m = (i * 4 + a * 2 + b, a * 4 + i * 2 + b, a * 4 + b * 2 + i)[d]
            coarse[m] = coarse[m] + t[i * el : (i + 1) * el]

    for c in range(4):
        p = (c // 2) * n + c % 2
        add(2, c, pair_update(n, 2, gather(f_ref, n, 2, p), None, mats["tz"][...], w_low, (zpen,)))

    finish(fine)
    half = (n * n) // 2
    for d, lo, hi, glo, ghi in ((0, r_lo0, r_hi0, g0lo, g0hi), (1, r_lo1, r_hi1, g1lo, g1hi)):
        glo[...] = lo[...]
        ghi[...] = hi[...]
        nb = dot(mats[f"q{d}"][...], jnp.concatenate([pen_b, lo[half], hi[half]], axis=0))
        dp = (jnp.maximum(pen, nb[:el]), jnp.maximum(pen, nb[el:]))
        pens[2 * d] = dp[0]
        pens[2 * d + 1] = dp[1]
        for c in range(4):
            p = (c // 2) * n + c % 2
            add(d, c, pair_update(n, d, gather(f_ref, n, d, p), [lo[p // 2], hi[p // 2]],
                                  mats[f"t{d}{p % 2}"][...], w_low, dp))

    first = [coarse[m] * scale[m] for m in range(8)]
    w0, w1 = math.sqrt(0.5), math.sqrt(1.5)

    def traces(d, c):
        a, b = c // 2, c % 2
        m0 = (a * 2 + b, a * 4 + b, a * 4 + b * 2)[d]
        m1 = m0 + (4, 2, 1)[d]
        v, g = w0 * first[m0], w1 * first[m1]
        return m0, m1, v + g, v - g, g

    stacked = {}
    ccop = copies(4, cs_up0, cs_dn0, cs_up1, cs_dn1, cr_lo0, cr_hi0, cr_lo1, cr_hi1)
    for d, up, dn in ((1, cs_up1, cs_dn1), (0, cs_up0, cs_dn0)):
        for c in range(4):
            _, _, tr, tl, g = traces(d, c)
            stacked[d, c] = split(tl) + split(tr) + split(g)
        for h in range(2):
            t = dot(mats[f"c{d}"][...], jnp.concatenate(stacked[d, 2 * h] + stacked[d, 2 * h + 1], axis=0))
            up[h] = t[:el].astype(BF)
            dn[h] = t[el:].astype(BF)
        if d == 1:
            start_y(ccop)
        else:
            start_x(ccop, cr_lo0, cr_hi0)

    applied = [3.0 * ((m >> 2) + ((m >> 1) & 1) + (m & 1)) * first[m] for m in range(8)]

    def lift(m0, m1, fu, fd, ju, jd):
        applied[m0] = applied[m0] + w0 * (fu - fd)
        applied[m1] = applied[m1] + w1 * ((fu + fd) - 0.5 * (ju + jd))

    for c in range(4):
        m0, m1, tr, tl, g = traces(2, c)
        ju = tr - roll(tl, -1)
        fu = 12.0 * ju - 0.5 * (g + roll(g, -1))
        lift(m0, m1, fu, roll(fu, 1), ju, roll(ju, 1))
    finish(ccop)
    for d, lo, hi in ((0, cr_lo0, cr_hi0), (1, cr_lo1, cr_hi1)):
        for c in range(4):
            m0, m1, tr, tl, g = traces(d, c)
            t = dot(mats[f"s{d}{c % 2}"][...],
                    jnp.concatenate(stacked[d, c] + [lo[c // 2], hi[c // 2]], axis=0))
            ju = tr - t[:el]
            jd = t[2 * el : 3 * el] - tl
            fu = 12.0 * ju - 0.5 * (g + t[el : 2 * el])
            fd = 12.0 * jd - 0.5 * (t[3 * el :] + g)
            lift(m0, m1, fu, fd, ju, jd)
    for m in range(8):
        second[m] = first[m] + scale[m] * (coarse[m] - SCALING * applied[m])


def fine_kernel(n, names, src, f_ref, g0lo, g0hi, g1lo, g1hi, pens, second, deg, *refs):
    count = len(names)
    mats = dict(zip(names, refs[:count]))
    updated, residual, acc, masks = refs[count:]
    lx, ly = src.shape[1], src.shape[2]
    el = lx * ly
    degree = deg[...]
    for lv in range(n):
        masks[lv] = jnp.where(degree >= lv, 1.0, 0.0)
    pairs = n * n
    w = mats["w"][...]

    def sweep(d, lo, hi):
        dp = (pens[2 * d], pens[2 * d + 1])

        def one(p, par, q):
            t = pair_update(n, d, gather(f_ref, n, d, p), [lo[q], hi[q]], mats[f"t{d}{par}"][...], w, dp)
            base, step = rows_of(n, d, p)
            for i in range(n):
                part = t[i * el : (i + 1) * el]
                if d == 0:
                    acc[base + step * i] = part
                else:
                    acc[base + step * i] += part

        def body(q, carry):
            one(2 * q, 0, q)
            one(2 * q + 1, 1, q)
            return carry

        lax.fori_loop(0, pairs // 2, body, 0, unroll=2)
        one(pairs - 1, 0, pairs // 2)

    sweep(0, g0lo, g0hi)
    sweep(1, g1lo, g1hi)
    zpen = (pens[4],)

    def body(p, carry):
        field = gather(f_ref, n, 2, p)
        t = pair_update(n, 2, field, None, mats["tz"][...], w, zpen)
        top = jnp.maximum(p // n, p % n)
        for k in range(n):
            m = p * n + k
            s = jnp.concatenate([src[m, x] for x in range(lx)], axis=0).astype(F32)
            r = masks[jnp.maximum(top, k)] * (s + acc[m] + t[k * el : (k + 1) * el])
            v = field[k].astype(F32)
            for x in range(lx):
                residual[m, x] = r[x * ly : (x + 1) * ly].astype(BF)
                updated[m, x] = v[x * ly : (x + 1) * ly]
        return carry

    lax.fori_loop(0, pairs, body, 0, unroll=2)
    for c in range(8):
        m = (c >> 2) * n * n + ((c >> 1) & 1) * n + (c & 1)
        v = f_ref[m].astype(F32) + second[c]
        for x in range(lx):
            updated[m, x] = v[x * ly : (x + 1) * ly]


def per_device(solution, source, degree):
    n = solution.shape[0]
    lx, ly, ez = solution.shape[3:]
    el, cubed, half = lx * ly, n * n * n, (n * n) // 2 + 1
    mats = matrices(n, lx, ly)
    single = [0.0 + 2.0 * 12.0 * 0.5, 3.0 + 2.0 * (12.0 * 1.5 - 1.5)]
    scale = [
        0.5 / (SCALING * (single[m >> 2] + single[(m >> 1) & 1] + single[m & 1])) for m in range(8)
    ]
    sol = solution.reshape(cubed, lx, ly, ez)
    src = source.reshape(cubed, lx, ly, ez)
    deg = degree.reshape(el, ez)
    srcc = source[:2, :2, :2].reshape(8, el, ez)
    vmem = pl.BlockSpec(memory_space=pltpu.VMEM)
    names = sorted(mats)
    sd = jax.ShapeDtypeStruct
    ghost = (half, el, ez)
    small = (2, el, ez)
    outs = pl.pallas_call(
        functools.partial(exchange_kernel, n, names, scale),
        out_shape=[sd((cubed, el, ez), BF)] + [sd(ghost, BF)] * 4 + [sd((6, el, ez), F32), sd((8, el, ez), F32)],
        in_specs=[vmem] * (3 + len(names)),
        out_specs=[vmem] * 7,
        scratch_shapes=[pltpu.VMEM(ghost, BF)] * 8 + [pltpu.VMEM(small, BF)] * 8
        + [pltpu.SemaphoreType.DMA((8,)), pltpu.SemaphoreType.DMA((8,))],
        compiler_params=pltpu.CompilerParams(
            collective_id=0, has_side_effects=True, vmem_limit_bytes=40 << 20
        ),
        name="exchange",
    )(sol, deg, srcc, *[jnp.asarray(mats[k]) for k in names])
    fnames = ["t00", "t01", "t10", "t11", "tz", "w"]
    updated, residual = pl.pallas_call(
        functools.partial(fine_kernel, n, fnames),
        out_shape=[sd((cubed, lx, ly, ez), F32), sd((cubed, lx, ly, ez), BF)],
        in_specs=[vmem] * (9 + len(fnames)),
        out_specs=[vmem] * 2,
        scratch_shapes=[pltpu.VMEM((cubed, el, ez), F32), pltpu.VMEM((n, el, ez), F32)],
        compiler_params=pltpu.CompilerParams(vmem_limit_bytes=48 << 20),
        name="fine",
    )(src, *outs, deg, *[jnp.asarray(mats[k]) for k in fnames])
    return updated.reshape(solution.shape), residual.reshape(solution.shape)


def solution(mesh):
    spec = P(None, None, None, "mem", "grp", None)
    return jax.shard_map(
        per_device,
        mesh=mesh,
        in_specs=(spec, spec, P("mem", "grp", None)),
        out_specs=(spec, spec),
        check_vma=False,
    )
```

```python
import functools
import math

import jax
import jax.numpy as jnp
import numpy as np
from jax import lax
from jax.experimental import pallas as pl
from jax.experimental.pallas import tpu as pltpu
from jax.sharding import PartitionSpec as P

BF = jnp.bfloat16
F32 = jnp.float32
SCALING = 0.00390625
MESH = pl.DeviceIdType.MESH


def tables(n):
    i = np.arange(n)
    w = np.sqrt((2.0 * i + 1.0) / 2.0)
    alt = np.where(i % 2 == 0, 1.0, -1.0)
    s = i * (i + 1.0) / 2.0
    low = np.minimum(i[:, None], i[None, :]).astype(np.float64)
    even = (i[:, None] + i[None, :]) % 2 == 0
    k = np.sqrt((2.0 * i[:, None] + 1.0) * (2.0 * i[None, :] + 1.0)) / 2.0 * low * (low + 1.0) * even
    listed = (w, w * alt, w * s, -w * alt * s, k)
    return [t.astype(np.float32).astype(BF).astype(np.float64) for t in listed]


def place(lx, ly, direction):
    e = np.arange(lx * ly)
    x, y = e // ly, e % ly
    if direction == 0:
        return x, lx, ly, y
    return y, ly, 1, x


def matrices(n, lx, ly):
    right, left, rs, ls, k = tables(n)
    el = lx * ly
    eye = np.eye(el)
    out = {}
    for d in range(2):
        c, count, stride, other = place(lx, ly, d)
        g = el // count
        up = np.zeros((el, el))
        dn = np.zeros((el, el))
        hi = np.zeros((el, g))
        lo = np.zeros((el, g))
        for e in range(el):
            if c[e] < count - 1:
                up[e, e + stride] = 1.0
            else:
                hi[e, other[e]] = 1.0
            if c[e] > 0:
                dn[e, e - stride] = 1.0
            else:
                lo[e, other[e]] = 1.0
        z = np.zeros((el, g))
        for par in range(2):
            def slab(a, b, par=par):
                pad = np.zeros((el, 2 * g))
                both = np.concatenate([a, b], axis=1)
                return np.concatenate([both, pad] if par == 0 else [pad, both], axis=1)

            none = slab(z, z)
            rows = [
                [np.kron(right, eye) - np.kron(left, up), none, slab(-hi, z)],
                [0.5 * (np.kron(rs, eye) + np.kron(ls, up)), none, slab(z, 0.5 * hi)],
                [np.kron(right, dn) - np.kron(left, eye), slab(lo, z), none],
                [0.5 * (np.kron(rs, dn) + np.kron(ls, eye)), slab(z, 0.5 * lo), none],
            ]
            out[f"t{d}{par}"] = np.block(rows)
            q = np.zeros((el, el))
            rows = [
                [up, up, q, q, q, q, none, slab(hi, z)],
                [q, q, q, q, up, up, none, slab(z, hi)],
                [q, q, dn, dn, q, q, slab(lo, z), none],
                [q, q, q, q, dn, dn, slab(z, lo), none],
            ]
            out[f"s{d}{par}"] = np.block(rows)
        eh, elow = hi.T, lo.T
        zz = np.zeros((2 * g, n * el))
        u = np.concatenate([np.kron(right, eh), np.kron(rs, eh)])
        v = np.concatenate([np.kron(left, elow), np.kron(ls, elow)])
        out[f"e{d}"] = np.block([[u, zz], [zz, u], [v, zz], [zz, v]])
        zp = np.zeros((2 * g, el))
        ph = np.concatenate([eh, np.zeros((g, el))])
        plo = np.concatenate([elow, np.zeros((g, el))])
        out[f"f{d}"] = np.block([[u, zp], [zz, ph], [v, zp], [zz, plo]])
        qz = np.zeros((el, 2 * g))
        none = np.zeros((el, 4 * g))
        out[f"q{d}"] = np.block(
            [
                [up, none, np.concatenate([qz, hi, z], axis=1)],
                [dn, np.concatenate([qz, lo, z], axis=1), none],
            ]
        )
        o = np.zeros((g, el))
        cu = np.block([[o, o, eh, eh, o, o], [o, o, o, o, eh, eh]])
        cd = np.block([[elow, elow, o, o, o, o], [o, o, o, o, elow, elow]])
        cz = np.zeros_like(cu)
        out[f"c{d}"] = np.block([[cu, cz], [cz, cu], [cd, cz], [cz, cd]])
    out["tz"] = np.concatenate(
        [np.kron(right, eye), np.kron(0.5 * rs, eye), np.kron(left, eye), np.kron(0.5 * ls, eye)]
    )
    ju = -0.5 * np.kron(rs[:, None], eye)
    fu = np.kron(right[:, None], eye)
    jd = -0.5 * np.kron(ls[:, None], eye)
    fd = -np.kron(left[:, None], eye)
    out["w"] = -SCALING * np.concatenate(
        [np.kron(k, eye), ju, ju, fu, fu, jd, jd, fd, fd], axis=1
    )
    return {name: m.astype(np.float32).astype(BF) for name, m in out.items()}


def dot(a, b):
    return jnp.dot(a, b, preferred_element_type=F32)


def split(v):
    hi = v.astype(BF)
    return [hi, (v - hi.astype(F32)).astype(BF)]


def roll(v, shift):
    return pltpu.roll(v, shift % v.shape[1], 1)


def rows_of(n, d, p):
    if d == 0:
        return p, n * n
    if d == 1:
        return (p // n) * (n * n) + p % n, n
    return p * n, 1


def gather(f_ref, n, d, p):
    base, step = rows_of(n, d, p)
    return [f_ref[base + step * i] for i in range(n)]


def mean_jump(t, el):
    return (t[a * el : (a + 1) * el] for a in range(4))


def sweep(n, d, f_ref, pairs, ghosts, tmats, w, pens):
    el = f_ref.shape[1]
    fields = [gather(f_ref, n, d, p) for p in pairs]
    if d < 2:
        lo, hi = ghosts
        firsts = [
            dot(tmats[p % 2], jnp.concatenate(field + [lo[p // 2], hi[p // 2]], axis=0))
            for p, field in zip(pairs, fields)
        ]
    else:
        firsts = [dot(tmats[0], jnp.concatenate(field, axis=0)) for field in fields]
    faces = []
    for t in firsts:
        if d < 2:
            ju, mu, jd, md = mean_jump(t, el)
            fu = pens[0] * ju - mu
            fd = pens[1] * jd - md
            faces.append(split(ju) + split(fu) + split(jd) + split(fd))
        else:
            tr, gr, tl, gl = mean_jump(t, el)
            ju = tr - roll(tl, -1)
            fu = pens[0] * ju - (gr + roll(gl, -1))
            faces.append(split(ju) + split(fu) + split(roll(ju, 1)) + split(roll(fu, 1)))
    return [dot(w, jnp.concatenate(field + face, axis=0)) for field, face in zip(fields, faces)]


def batches(total, size):
    return [list(range(a, min(a + size, total))) for a in range(0, total, size)]


def exchange_kernel(n, slots, scale, sol, src, deg, packed, f_ref, acc, g1lo, g1hi, pens, second,
                    s_up0, s_dn0, s_up1, s_dn1, r_lo0, r_hi0, r_lo1, r_hi1,
                    cs_up0, cs_dn0, cs_up1, cs_dn1, cr_lo0, cr_hi0, cr_lo1, cr_hi1, send, recv):
    def mat(name):
        off, rows, cols = slots[name]
        return packed[off : off + rows, :cols]

    mem, grp = lax.axis_index("mem"), lax.axis_index("grp")
    nmem, ngrp = lax.axis_size("mem"), lax.axis_size("grp")
    below = {"grp": grp, "mem": jnp.maximum(mem - 1, 0)}
    above = {"grp": grp, "mem": jnp.minimum(mem + 1, nmem - 1)}
    south = {"grp": lax.rem(grp + ngrp - 1, ngrp), "mem": mem}
    north = {"grp": lax.rem(grp + 1, ngrp), "mem": mem}
    has_lo, has_hi = mem > 0, mem < nmem - 1
    lx, ly = sol.shape[1], sol.shape[2]
    el = lx * ly
    cubed, pairs, half = n * n * n, n * n, (n * n) // 2

    barrier = pltpu.get_barrier_semaphore()

    @pl.when(has_lo)
    def _():
        pl.semaphore_signal(barrier, inc=1, device_id=below, device_id_type=MESH)

    @pl.when(has_hi)
    def _():
        pl.semaphore_signal(barrier, inc=1, device_id=above, device_id_type=MESH)

    pl.semaphore_signal(barrier, inc=1, device_id=south, device_id_type=MESH)
    pl.semaphore_signal(barrier, inc=1, device_id=north, device_id_type=MESH)

    degree = jnp.concatenate([deg[x] for x in range(lx)], axis=0)
    masks = {lv: jnp.where(degree >= lv, 1.0, 0.0).astype(BF) for lv in range(3, n)}
    for m in range(cubed):
        f_ref[m] = jnp.concatenate([sol[m, x] for x in range(lx)], axis=0)
    for m in range(cubed):
        top = max(m // pairs, (m // n) % n, m % n)
        if top > 2:
            f_ref[m] = f_ref[m] * masks[top]

    pen = (3 * (degree + 1) * (degree + 1)).astype(F32)
    pen_b = pen.astype(BF)

    def edges(d, up, dn):
        e = mat(f"e{d}")
        out = [
            dot(e, jnp.concatenate(gather(f_ref, n, d, 2 * q) + gather(f_ref, n, d, 2 * q + 1), axis=0))
            for q in range(half)
        ]
        out.append(dot(mat(f"f{d}"), jnp.concatenate(gather(f_ref, n, d, pairs - 1) + [pen_b], axis=0)))
        for q, t in enumerate(out):
            up[q] = t[:el].astype(BF)
            dn[q] = t[el:].astype(BF)

    def copies(base, up0, dn0, up1, dn1, lo0, hi0, lo1, hi1):
        def mk(a, b, k, to):
            return pltpu.make_async_remote_copy(
                src_ref=a, dst_ref=b, send_sem=send.at[base + k], recv_sem=recv.at[base + k],
                device_id=to, device_id_type=MESH,
            )

        return (mk(up1, lo1, 2, north), mk(dn1, hi1, 3, south), mk(up0, lo0, 0, above), mk(dn0, hi0, 1, below))

    def start_y(c):
        c[0].start()
        c[1].start()

    def start_x(c, lo, hi):
        @pl.when(has_hi)
        def _():
            c[2].start()

        @pl.when(has_lo)
        def _():
            c[3].start()

        @pl.when(jnp.logical_not(has_lo))
        def _():
            lo[...] = jnp.zeros_like(lo)

        @pl.when(jnp.logical_not(has_hi))
        def _():
            hi[...] = jnp.zeros_like(hi)

    def finish(c):
        c[0].wait()
        c[1].wait()

        @pl.when(has_hi)
        def _():
            c[2].wait_send()
            c[3].wait_recv()

        @pl.when(has_lo)
        def _():
            c[3].wait_send()
            c[2].wait_recv()

    fine = copies(0, s_up0, s_dn0, s_up1, s_dn1, r_lo0, r_hi0, r_lo1, r_hi1)
    edges(1, s_up1, s_dn1)
    pl.semaphore_wait(barrier, 2 + has_lo.astype(jnp.int32) + has_hi.astype(jnp.int32))
    start_y(fine)
    edges(0, s_up0, s_dn0)
    start_x(fine, r_lo0, r_hi0)

    w = mat("w")
    w_low = w[: 2 * el]
    zpen = jnp.maximum(pen, roll(pen, -1))
    for m in range(cubed):
        for x in range(lx):
            acc[m, x * ly : (x + 1) * ly] = src[m, x].astype(F32)
    for batch in batches(pairs, ZBATCH):
        for p, t in zip(batch, sweep(n, 2, f_ref, batch, None, [mat("tz")], w, (zpen,))):
            for k in range(n):
                acc[p * n + k] += t[k * el : (k + 1) * el]

    finish(fine)
    low = [(c // 2) * n + c % 2 for c in range(4)]
    corner = [(m >> 2) * pairs + ((m >> 1) & 1) * n + (m & 1) for m in range(8)]
    coarse = [acc[m] for m in corner]
    xpen = None
    xmats = [mat("t00"), mat("t01")]
    for d, lo, hi in ((0, r_lo0, r_hi0), (1, r_lo1, r_hi1)):
        nb = dot(mat(f"q{d}"), jnp.concatenate([pen_b, lo[half], hi[half]], axis=0))
        dp = (jnp.maximum(pen, nb[:el]), jnp.maximum(pen, nb[el:]))
        if d == 0:
            xpen = dp
        else:
            pens[0] = dp[0]
            pens[1] = dp[1]
        tm = [mat(f"t{d}0"), mat(f"t{d}1")]
        for c, t in enumerate(sweep(n, d, f_ref, low, (lo, hi), tm, w_low, dp)):
            a, b = c // 2, c % 2
            for i in range(2):
                m = (i * 4 + a * 2 + b, a * 4 + i * 2 + b)[d]
                coarse[m] = coarse[m] + t[i * el : (i + 1) * el]

    first = [coarse[m] * scale[m] for m in range(8)]
    w0, w1 = math.sqrt(0.5), math.sqrt(1.5)

    def traces(d, c):
        a, b = c // 2, c % 2
        m0 = (a * 2 + b, a * 4 + b, a * 4 + b * 2)[d]
        m1 = m0 + (4, 2, 1)[d]
        v, g = w0 * first[m0], w1 * first[m1]
        return m0, m1, v + g, v - g, g

    stacked = {}
    ccop = copies(4, cs_up0, cs_dn0, cs_up1, cs_dn1, cr_lo0, cr_hi0, cr_lo1, cr_hi1)
    for d, up, dn in ((1, cs_up1, cs_dn1), (0, cs_up0, cs_dn0)):
        for c in range(4):
            _, _, tr, tl, g = traces(d, c)
            stacked[d, c] = split(tl) + split(tr) + split(g)
        for h in range(2):
            t = dot(mat(f"c{d}"), jnp.concatenate(stacked[d, 2 * h] + stacked[d, 2 * h + 1], axis=0))
            up[h] = t[:el].astype(BF)
            dn[h] = t[el:].astype(BF)
        if d == 1:
            start_y(ccop)
        else:
            start_x(ccop, cr_lo0, cr_hi0)

    for batch in batches(pairs, XBATCH):
        for p, t in zip(batch, sweep(n, 0, f_ref, batch, (r_lo0, r_hi0), xmats, w, xpen)):
            for i in range(n):
                acc[p + pairs * i] += t[i * el : (i + 1) * el]
    g1lo[...] = r_lo1[...]
    g1hi[...] = r_hi1[...]

    applied = [3.0 * ((m >> 2) + ((m >> 1) & 1) + (m & 1)) * first[m] for m in range(8)]

    def lift(m0, m1, fu, fd, ju, jd):
        applied[m0] = applied[m0] + w0 * (fu - fd)
        applied[m1] = applied[m1] + w1 * ((fu + fd) - 0.5 * (ju + jd))

    for c in range(4):
        m0, m1, tr, tl, g = traces(2, c)
        ju = tr - roll(tl, -1)
        fu = 12.0 * ju - 0.5 * (g + roll(g, -1))
        lift(m0, m1, fu, roll(fu, 1), ju, roll(ju, 1))
    finish(ccop)
    for d, lo, hi in ((0, cr_lo0, cr_hi0), (1, cr_lo1, cr_hi1)):
        for c in range(4):
            m0, m1, tr, tl, g = traces(d, c)
            t = dot(mat(f"s{d}{c % 2}"),
                    jnp.concatenate(stacked[d, c] + [lo[c // 2], hi[c // 2]], axis=0))
            ju = tr - t[:el]
            jd = t[2 * el : 3 * el] - tl
            fu = 12.0 * ju - 0.5 * (g + t[el : 2 * el])
            fd = 12.0 * jd - 0.5 * (t[3 * el :] + g)
            lift(m0, m1, fu, fd, ju, jd)
    for m in range(8):
        second[m] = first[m] + scale[m] * (coarse[m] - SCALING * applied[m])


def fine_kernel(n, slots, f_ref, acc, g1lo, g1hi, pens, second, deg, packed, updated, residual,
                ubuf, rbuf, usem, rsem):
    def mat(name):
        off, rows, cols = slots[name]
        return packed[off : off + rows, :cols]

    lx, ly = ubuf.shape[1], ubuf.shape[2]
    el = lx * ly
    cubed, pairs = n * n * n, n * n
    degree = jnp.concatenate([deg[x] for x in range(lx)], axis=0)
    masks = {lv: jnp.where(degree >= lv, 1.0, 0.0) for lv in range(3, n)}
    corner = {(m >> 2) * pairs + ((m >> 1) & 1) * n + (m & 1): m for m in range(8)}
    out_u = pltpu.make_async_copy(ubuf, updated, usem)
    for m in range(cubed):
        v = f_ref[m].astype(F32)
        if m in corner:
            v = v + second[corner[m]]
        for x in range(lx):
            ubuf[m, x] = v[x * ly : (x + 1) * ly]
    out_u.start()
    tm = [mat("t10"), mat("t11")]
    dp = (pens[0], pens[1])
    out_r = []
    for batch in batches(pairs, YBATCH):
        for p, t in zip(batch, sweep(n, 1, f_ref, batch, (g1lo, g1hi), tm, mat("w"), dp)):
            i, k = p // n, p % n
            for j in range(n):
                m = i * pairs + j * n + k
                r = acc[m] + t[j * el : (j + 1) * el]
                top = max(i, j, k)
                if top > 2:
                    r = masks[top] * r
                r = r.astype(BF)
                for x in range(lx):
                    rbuf[m, x] = r[x * ly : (x + 1) * ly]
            if k == n - 1:
                part = pl.ds(i * pairs, pairs)
                out_r.append(pltpu.make_async_copy(rbuf.at[part], residual.at[part], rsem.at[i]))
                out_r[-1].start()
    for c in out_r:
        c.wait()
    out_u.wait()


ZBATCH = 49
XBATCH = 49
YBATCH = 49


def pack(mats):
    slots, parts, off = {}, [], 0
    for name in sorted(mats):
        m = mats[name]
        slots[name] = (off, m.shape[0], m.shape[1])
        rows = -(-m.shape[0] // 16) * 16
        parts.append(np.pad(m, ((0, rows - m.shape[0]), (0, 256 - m.shape[1]))))
        off += rows
    return slots, np.concatenate(parts)


def per_device(solution, source, degree):
    n = solution.shape[0]
    lx, ly, ez = solution.shape[3:]
    el, cubed, half = lx * ly, n * n * n, (n * n) // 2 + 1
    slots, packed = pack(matrices(n, lx, ly))
    packed = jnp.asarray(packed)
    single = [0.0 + 2.0 * 12.0 * 0.5, 3.0 + 2.0 * (12.0 * 1.5 - 1.5)]
    scale = [
        0.5 / (SCALING * (single[m >> 2] + single[(m >> 1) & 1] + single[m & 1])) for m in range(8)
    ]
    sol = solution.reshape(cubed, lx, ly, ez)
    src = source.reshape(cubed, lx, ly, ez)
    vmem = pl.BlockSpec(memory_space=pltpu.VMEM)
    hbm = pl.BlockSpec(memory_space=pl.ANY)
    sd = jax.ShapeDtypeStruct
    ghost = (half, el, ez)
    small = (2, el, ez)
    outs = pl.pallas_call(
        functools.partial(exchange_kernel, n, slots, scale),
        out_shape=[sd((cubed, el, ez), BF), sd((cubed, el, ez), F32), sd(ghost, BF), sd(ghost, BF),
                   sd((2, el, ez), F32), sd((8, el, ez), F32)],
        in_specs=[vmem] * 4,
        out_specs=[vmem] * 6,
        scratch_shapes=[pltpu.VMEM(ghost, BF)] * 8 + [pltpu.VMEM(small, BF)] * 8
        + [pltpu.SemaphoreType.DMA((8,)), pltpu.SemaphoreType.DMA((8,))],
        compiler_params=pltpu.CompilerParams(
            collective_id=0, has_side_effects=True, vmem_limit_bytes=34 << 20
        ),
        name="exchange",
    )(sol, src, degree, packed)
    updated, residual = pl.pallas_call(
        functools.partial(fine_kernel, n, slots),
        out_shape=[sd((cubed, lx, ly, ez), F32), sd((cubed, lx, ly, ez), BF)],
        in_specs=[vmem] * 8,
        out_specs=[hbm] * 2,
        scratch_shapes=[pltpu.VMEM((cubed, lx, ly, ez), F32), pltpu.VMEM((cubed, lx, ly, ez), BF),
                        pltpu.SemaphoreType.DMA, pltpu.SemaphoreType.DMA((n,))],
        compiler_params=pltpu.CompilerParams(vmem_limit_bytes=34 << 20),
        name="fine",
    )(*outs, degree, packed)
    return updated.reshape(solution.shape), residual.reshape(solution.shape)


def solution(mesh):
    spec = P(None, None, None, "mem", "grp", None)
    return jax.shard_map(
        per_device,
        mesh=mesh,
        in_specs=(spec, spec, P("mem", "grp", None)),
        out_specs=(spec, spec),
        check_vma=False,
    )
```

```python
import functools
import math

import jax
import jax.numpy as jnp
import numpy as np
from jax import lax
from jax.experimental import pallas as pl
from jax.experimental.pallas import tpu as pltpu
from jax.sharding import PartitionSpec as P

BF = jnp.bfloat16
F32 = jnp.float32
SCALING = 0.00390625
MESH = pl.DeviceIdType.MESH


def tables(n):
    i = np.arange(n)
    w = np.sqrt((2.0 * i + 1.0) / 2.0)
    alt = np.where(i % 2 == 0, 1.0, -1.0)
    s = i * (i + 1.0) / 2.0
    low = np.minimum(i[:, None], i[None, :]).astype(np.float64)
    even = (i[:, None] + i[None, :]) % 2 == 0
    k = np.sqrt((2.0 * i[:, None] + 1.0) * (2.0 * i[None, :] + 1.0)) / 2.0 * low * (low + 1.0) * even
    listed = (w, w * alt, w * s, -w * alt * s, k)
    return [t.astype(np.float32).astype(BF).astype(np.float64) for t in listed]


def place(lx, ly, direction):
    e = np.arange(lx * ly)
    x, y = e // ly, e % ly
    if direction == 0:
        return x, lx, ly, y
    return y, ly, 1, x


def matrices(n, lx, ly):
    right, left, rs, ls, k = tables(n)
    el = lx * ly
    eye = np.eye(el)
    out = {}
    for d in range(2):
        c, count, stride, other = place(lx, ly, d)
        g = el // count
        up = np.zeros((el, el))
        dn = np.zeros((el, el))
        hi = np.zeros((el, g))
        lo = np.zeros((el, g))
        for e in range(el):
            if c[e] < count - 1:
                up[e, e + stride] = 1.0
            else:
                hi[e, other[e]] = 1.0
            if c[e] > 0:
                dn[e, e - stride] = 1.0
            else:
                lo[e, other[e]] = 1.0
        z = np.zeros((el, g))
        for par in range(2):
            def slab(a, b, par=par):
                pad = np.zeros((el, 2 * g))
                both = np.concatenate([a, b], axis=1)
                return np.concatenate([both, pad] if par == 0 else [pad, both], axis=1)

            none = slab(z, z)
            rows = [
                [np.kron(right, eye) - np.kron(left, up), none, slab(-hi, z)],
                [0.5 * (np.kron(rs, eye) + np.kron(ls, up)), none, slab(z, 0.5 * hi)],
                [np.kron(right, dn) - np.kron(left, eye), slab(lo, z), none],
                [0.5 * (np.kron(rs, dn) + np.kron(ls, eye)), slab(z, 0.5 * lo), none],
            ]
            out[f"t{d}{par}"] = np.block(rows)
            q = np.zeros((el, el))
            rows = [
                [up, up, q, q, q, q, none, slab(hi, z)],
                [q, q, q, q, up, up, none, slab(z, hi)],
                [q, q, dn, dn, q, q, slab(lo, z), none],
                [q, q, q, q, dn, dn, slab(z, lo), none],
            ]
            out[f"s{d}{par}"] = np.block(rows)
        eh, elow = hi.T, lo.T
        zz = np.zeros((2 * g, n * el))
        u = np.concatenate([np.kron(right, eh), np.kron(rs, eh)])
        v = np.concatenate([np.kron(left, elow), np.kron(ls, elow)])
        out[f"e{d}"] = np.block([[u, zz], [zz, u], [v, zz], [zz, v]])
        zp = np.zeros((2 * g, el))
        ph = np.concatenate([eh, np.zeros((g, el))])
        plo = np.concatenate([elow, np.zeros((g, el))])
        out[f"f{d}"] = np.block([[u, zp], [zz, ph], [v, zp], [zz, plo]])
        qz = np.zeros((el, 2 * g))
        none = np.zeros((el, 4 * g))
        out[f"q{d}"] = np.block(
            [
                [up, none, np.concatenate([qz, hi, z], axis=1)],
                [dn, np.concatenate([qz, lo, z], axis=1), none],
            ]
        )
        o = np.zeros((g, el))
        cu = np.block([[o, o, eh, eh, o, o], [o, o, o, o, eh, eh]])
        cd = np.block([[elow, elow, o, o, o, o], [o, o, o, o, elow, elow]])
        cz = np.zeros_like(cu)
        out[f"c{d}"] = np.block([[cu, cz], [cz, cu], [cd, cz], [cz, cd]])
    out["tz"] = np.concatenate(
        [np.kron(right, eye), np.kron(0.5 * rs, eye), np.kron(left, eye), np.kron(0.5 * ls, eye)]
    )
    ju = -0.5 * np.kron(rs[:, None], eye)
    fu = np.kron(right[:, None], eye)
    jd = -0.5 * np.kron(ls[:, None], eye)
    fd = -np.kron(left[:, None], eye)
    out["w"] = -SCALING * np.concatenate(
        [np.kron(k, eye), ju, ju, fu, fu, jd, jd, fd, fd], axis=1
    )
    return {name: m.astype(np.float32).astype(BF) for name, m in out.items()}


def dot(a, b):
    return jnp.dot(a, b, preferred_element_type=F32)


def split(v):
    hi = v.astype(BF)
    return [hi, (v - hi.astype(F32)).astype(BF)]


def roll(v, shift):
    return pltpu.roll(v, shift % v.shape[1], 1)


def rows_of(n, d, p):
    if d == 0:
        return p, n * n
    if d == 1:
        return (p // n) * (n * n) + p % n, n
    return p * n, 1


def gather(f_ref, n, d, p):
    base, step = rows_of(n, d, p)
    return [f_ref[base + step * i] for i in range(n)]


def mean_jump(t, el):
    return (t[a * el : (a + 1) * el] for a in range(4))


def sweep(n, d, f_ref, pairs, ghosts, tmats, w, pens):
    el = f_ref.shape[1]
    fields = [gather(f_ref, n, d, p) for p in pairs]
    if d < 2:
        lo, hi = ghosts
        firsts = [
            dot(tmats[p % 2], jnp.concatenate(field + [lo[p // 2], hi[p // 2]], axis=0))
            for p, field in zip(pairs, fields)
        ]
    else:
        firsts = [dot(tmats[0], jnp.concatenate(field, axis=0)) for field in fields]
    faces = []
    for t in firsts:
        if d < 2:
            ju, mu, jd, md = mean_jump(t, el)
            fu = pens[0] * ju - mu
            fd = pens[1] * jd - md
            faces.append(split(ju) + split(fu) + split(jd) + split(fd))
        else:
            tr, gr, tl, gl = mean_jump(t, el)
            ju = tr - roll(tl, -1)
            fu = pens[0] * ju - (gr + roll(gl, -1))
            faces.append(split(ju) + split(fu) + split(roll(ju, 1)) + split(roll(fu, 1)))
    return [dot(w, jnp.concatenate(field + face, axis=0)) for field, face in zip(fields, faces)]


def batches(total, size):
    return [list(range(a, min(a + size, total))) for a in range(0, total, size)]


def exchange_kernel(n, slots, scale, sol_h, src_h, deg_h, packed_h, f_ref, acc_h, g1lo, g1hi, pens, second,
                    s_up0, s_dn0, s_up1, s_dn1, r_lo0, r_hi0, r_lo1, r_hi1,
                    cs_up0, cs_dn0, cs_up1, cs_dn1, cr_lo0, cr_hi0, cr_lo1, cr_hi1, send, recv,
                    sol, src, deg, packed, s_ref, acc, asem, isem):
    def mat(name):
        off, rows, cols = slots[name]
        return packed[off : off + rows, :cols]

    mem, grp = lax.axis_index("mem"), lax.axis_index("grp")
    nmem, ngrp = lax.axis_size("mem"), lax.axis_size("grp")
    below = {"grp": grp, "mem": jnp.maximum(mem - 1, 0)}
    above = {"grp": grp, "mem": jnp.minimum(mem + 1, nmem - 1)}
    south = {"grp": lax.rem(grp + ngrp - 1, ngrp), "mem": mem}
    north = {"grp": lax.rem(grp + 1, ngrp), "mem": mem}
    has_lo, has_hi = mem > 0, mem < nmem - 1
    lx, ly = sol_h.shape[1], sol_h.shape[2]
    el = lx * ly
    cubed, pairs, half = n * n * n, n * n, (n * n) // 2

    loads = [pltpu.make_async_copy(deg_h, deg, isem.at[0]), pltpu.make_async_copy(packed_h, packed, isem.at[1])]
    for i in range(n):
        part = pl.ds(i * pairs, pairs)
        loads.append(pltpu.make_async_copy(sol_h.at[part], sol.at[part], isem.at[2 + i]))
    loads.append(pltpu.make_async_copy(src_h, src, isem.at[2 + n]))
    for c in [loads[0]] + loads[2 : 2 + n] + [loads[1], loads[2 + n]]:
        c.start()

    barrier = pltpu.get_barrier_semaphore()

    @pl.when(has_lo)
    def _():
        pl.semaphore_signal(barrier, inc=1, device_id=below, device_id_type=MESH)

    @pl.when(has_hi)
    def _():
        pl.semaphore_signal(barrier, inc=1, device_id=above, device_id_type=MESH)

    pl.semaphore_signal(barrier, inc=1, device_id=south, device_id_type=MESH)
    pl.semaphore_signal(barrier, inc=1, device_id=north, device_id_type=MESH)

    loads[0].wait()
    degree = jnp.concatenate([deg[x] for x in range(lx)], axis=0)
    masks = {lv: jnp.where(degree >= lv, 1.0, 0.0).astype(BF) for lv in range(3, n)}
    for m in range(cubed):
        if m % pairs == 0:
            loads[2 + m // pairs].wait()
        f_ref[m] = jnp.concatenate([sol[m, x] for x in range(lx)], axis=0)
    for m in range(cubed):
        top = max(m // pairs, (m // n) % n, m % n)
        if top > 2:
            f_ref[m] = f_ref[m] * masks[top]

    pen = (3 * (degree + 1) * (degree + 1)).astype(F32)
    pen_b = pen.astype(BF)

    def edges(d, up, dn):
        e = mat(f"e{d}")
        out = [
            dot(e, jnp.concatenate(gather(f_ref, n, d, 2 * q) + gather(f_ref, n, d, 2 * q + 1), axis=0))
            for q in range(half)
        ]
        out.append(dot(mat(f"f{d}"), jnp.concatenate(gather(f_ref, n, d, pairs - 1) + [pen_b], axis=0)))
        for q, t in enumerate(out):
            up[q] = t[:el].astype(BF)
            dn[q] = t[el:].astype(BF)

    def copies(base, up0, dn0, up1, dn1, lo0, hi0, lo1, hi1):
        def mk(a, b, k, to):
            return pltpu.make_async_remote_copy(
                src_ref=a, dst_ref=b, send_sem=send.at[base + k], recv_sem=recv.at[base + k],
                device_id=to, device_id_type=MESH,
            )

        return (mk(up1, lo1, 2, north), mk(dn1, hi1, 3, south), mk(up0, lo0, 0, above), mk(dn0, hi0, 1, below))

    def start_y(c):
        c[0].start()
        c[1].start()

    def start_x(c, lo, hi):
        @pl.when(has_hi)
        def _():
            c[2].start()

        @pl.when(has_lo)
        def _():
            c[3].start()

        @pl.when(jnp.logical_not(has_lo))
        def _():
            lo[...] = jnp.zeros_like(lo)

        @pl.when(jnp.logical_not(has_hi))
        def _():
            hi[...] = jnp.zeros_like(hi)

    def finish(c):
        c[0].wait()
        c[1].wait()

        @pl.when(has_hi)
        def _():
            c[2].wait_send()
            c[3].wait_recv()

        @pl.when(has_lo)
        def _():
            c[3].wait_send()
            c[2].wait_recv()

    loads[1].wait()
    fine = copies(0, s_up0, s_dn0, s_up1, s_dn1, r_lo0, r_hi0, r_lo1, r_hi1)
    edges(1, s_up1, s_dn1)
    pl.semaphore_wait(barrier, 2 + has_lo.astype(jnp.int32) + has_hi.astype(jnp.int32))
    start_y(fine)
    edges(0, s_up0, s_dn0)
    start_x(fine, r_lo0, r_hi0)

    w = mat("w")
    w_low = w[: 2 * el]
    zpen = jnp.maximum(pen, roll(pen, -1))
    loads[2 + n].wait()
    for m in range(cubed):
        s_ref[m] = jnp.concatenate([src[m, x] for x in range(lx)], axis=0)
    for batch in batches(pairs, ZBATCH):
        for p, t in zip(batch, sweep(n, 2, f_ref, batch, None, [mat("tz")], w, (zpen,))):
            for k in range(n):
                acc[p * n + k] = s_ref[p * n + k].astype(F32) + t[k * el : (k + 1) * el]

    finish(fine)
    low = [(c // 2) * n + c % 2 for c in range(4)]
    corner = [(m >> 2) * pairs + ((m >> 1) & 1) * n + (m & 1) for m in range(8)]
    coarse = [acc[m] for m in corner]
    xpen = None
    xmats = [mat("t00"), mat("t01")]
    for d, lo, hi in ((0, r_lo0, r_hi0), (1, r_lo1, r_hi1)):
        nb = dot(mat(f"q{d}"), jnp.concatenate([pen_b, lo[half], hi[half]], axis=0))
        dp = (jnp.maximum(pen, nb[:el]), jnp.maximum(pen, nb[el:]))
        if d == 0:
            xpen = dp
        else:
            pens[0] = dp[0]
            pens[1] = dp[1]
        tm = [mat(f"t{d}0"), mat(f"t{d}1")]
        for c, t in enumerate(sweep(n, d, f_ref, low, (lo, hi), tm, w_low, dp)):
            a, b = c // 2, c % 2
            for i in range(2):
                m = (i * 4 + a * 2 + b, a * 4 + i * 2 + b)[d]
                coarse[m] = coarse[m] + t[i * el : (i + 1) * el]

    first = [coarse[m] * scale[m] for m in range(8)]
    w0, w1 = math.sqrt(0.5), math.sqrt(1.5)

    def traces(d, c):
        a, b = c // 2, c % 2
        m0 = (a * 2 + b, a * 4 + b, a * 4 + b * 2)[d]
        m1 = m0 + (4, 2, 1)[d]
        v, g = w0 * first[m0], w1 * first[m1]
        return m0, m1, v + g, v - g, g

    stacked = {}
    ccop = copies(4, cs_up0, cs_dn0, cs_up1, cs_dn1, cr_lo0, cr_hi0, cr_lo1, cr_hi1)
    for d, up, dn in ((1, cs_up1, cs_dn1), (0, cs_up0, cs_dn0)):
        for c in range(4):
            _, _, tr, tl, g = traces(d, c)
            stacked[d, c] = split(tl) + split(tr) + split(g)
        for h in range(2):
            t = dot(mat(f"c{d}"), jnp.concatenate(stacked[d, 2 * h] + stacked[d, 2 * h + 1], axis=0))
            up[h] = t[:el].astype(BF)
            dn[h] = t[el:].astype(BF)
        if d == 1:
            start_y(ccop)
        else:
            start_x(ccop, cr_lo0, cr_hi0)

    for batch in batches(pairs, XBATCH):
        for p, t in zip(batch, sweep(n, 0, f_ref, batch, (r_lo0, r_hi0), xmats, w, xpen)):
            for i in range(n):
                acc[p + pairs * i] += t[i * el : (i + 1) * el]
    acc_out = pltpu.make_async_copy(acc, acc_h, asem)
    acc_out.start()
    g1lo[...] = r_lo1[...]
    g1hi[...] = r_hi1[...]

    applied = [3.0 * ((m >> 2) + ((m >> 1) & 1) + (m & 1)) * first[m] for m in range(8)]

    def lift(m0, m1, fu, fd, ju, jd):
        applied[m0] = applied[m0] + w0 * (fu - fd)
        applied[m1] = applied[m1] + w1 * ((fu + fd) - 0.5 * (ju + jd))

    for c in range(4):
        m0, m1, tr, tl, g = traces(2, c)
        ju = tr - roll(tl, -1)
        fu = 12.0 * ju - 0.5 * (g + roll(g, -1))
        lift(m0, m1, fu, roll(fu, 1), ju, roll(ju, 1))
    finish(ccop)
    for d, lo, hi in ((0, cr_lo0, cr_hi0), (1, cr_lo1, cr_hi1)):
        for c in range(4):
            m0, m1, tr, tl, g = traces(d, c)
            t = dot(mat(f"s{d}{c % 2}"),
                    jnp.concatenate(stacked[d, c] + [lo[c // 2], hi[c // 2]], axis=0))
            ju = tr - t[:el]
            jd = t[2 * el : 3 * el] - tl
            fu = 12.0 * ju - 0.5 * (g + t[el : 2 * el])
            fd = 12.0 * jd - 0.5 * (t[3 * el :] + g)
            lift(m0, m1, fu, fd, ju, jd)
    for m in range(8):
        second[m] = first[m] + scale[m] * (coarse[m] - SCALING * applied[m])
    acc_out.wait()


def fine_kernel(n, slots, f_ref, acc_h, g1lo, g1hi, pens, second, deg, packed, updated, residual,
                ubuf, rbuf, acc, usem, rsem, asem):
    def mat(name):
        off, rows, cols = slots[name]
        return packed[off : off + rows, :cols]

    lx, ly = ubuf.shape[1], ubuf.shape[2]
    el = lx * ly
    cubed, pairs = n * n * n, n * n
    degree = jnp.concatenate([deg[x] for x in range(lx)], axis=0)
    masks = {lv: jnp.where(degree >= lv, 1.0, 0.0) for lv in range(3, n)}
    corner = {(m >> 2) * pairs + ((m >> 1) & 1) * n + (m & 1): m for m in range(8)}
    loads = []
    for i in range(n):
        part = pl.ds(i * pairs, pairs)
        loads.append(pltpu.make_async_copy(acc_h.at[part], acc.at[part], asem.at[i]))
        loads[-1].start()
    out_u = []
    for m in range(cubed):
        v = f_ref[m].astype(F32)
        if m in corner:
            v = v + second[corner[m]]
        for x in range(lx):
            ubuf[m, x] = v[x * ly : (x + 1) * ly]
        if m % pairs == pairs - 1:
            i = m // pairs
            part = pl.ds(i * pairs, pairs)
            out_u.append(pltpu.make_async_copy(ubuf.at[part], updated.at[part], usem.at[i]))
            out_u[-1].start()
    tm = [mat("t10"), mat("t11")]
    dp = (pens[0], pens[1])
    out_r = []
    for batch in batches(pairs, YBATCH):
        for p, t in zip(batch, sweep(n, 1, f_ref, batch, (g1lo, g1hi), tm, mat("w"), dp)):
            i, k = p // n, p % n
            if k == 0:
                loads[i].wait()
            for j in range(n):
                m = i * pairs + j * n + k
                r = acc[m] + t[j * el : (j + 1) * el]
                top = max(i, j, k)
                if top > 2:
                    r = masks[top] * r
                r = r.astype(BF)
                for x in range(lx):
                    rbuf[m, x] = r[x * ly : (x + 1) * ly]
            if k == n - 1:
                part = pl.ds(i * pairs, pairs)
                out_r.append(pltpu.make_async_copy(rbuf.at[part], residual.at[part], rsem.at[i]))
                out_r[-1].start()
    for c in out_u + out_r:
        c.wait()


ZBATCH = 49
XBATCH = 49
YBATCH = 49


def pack(mats):
    slots, parts, off = {}, [], 0
    for name in sorted(mats):
        m = mats[name]
        slots[name] = (off, m.shape[0], m.shape[1])
        rows = -(-m.shape[0] // 16) * 16
        parts.append(np.pad(m, ((0, rows - m.shape[0]), (0, 256 - m.shape[1]))))
        off += rows
    return slots, np.concatenate(parts)


def per_device(solution, source, degree):
    n = solution.shape[0]
    lx, ly, ez = solution.shape[3:]
    el, cubed, half = lx * ly, n * n * n, (n * n) // 2 + 1
    slots, packed = pack(matrices(n, lx, ly))
    packed = jnp.asarray(packed)
    single = [0.0 + 2.0 * 12.0 * 0.5, 3.0 + 2.0 * (12.0 * 1.5 - 1.5)]
    scale = [
        0.5 / (SCALING * (single[m >> 2] + single[(m >> 1) & 1] + single[m & 1])) for m in range(8)
    ]
    sol = solution.reshape(cubed, lx, ly, ez)
    src = source.reshape(cubed, lx, ly, ez)
    vmem = pl.BlockSpec(memory_space=pltpu.VMEM)
    hbm = pl.BlockSpec(memory_space=pl.ANY)
    sd = jax.ShapeDtypeStruct
    ghost = (half, el, ez)
    small = (2, el, ez)
    outs = pl.pallas_call(
        functools.partial(exchange_kernel, n, slots, scale),
        out_shape=[sd((cubed, el, ez), BF), sd((cubed, el, ez), F32), sd(ghost, BF), sd(ghost, BF),
                   sd((2, el, ez), F32), sd((8, el, ez), F32)],
        in_specs=[pl.BlockSpec(memory_space=pltpu.HBM)] * 4,
        out_specs=[vmem, hbm] + [vmem] * 4,
        scratch_shapes=[pltpu.VMEM(ghost, BF)] * 8 + [pltpu.VMEM(small, BF)] * 8
        + [pltpu.SemaphoreType.DMA((8,)), pltpu.SemaphoreType.DMA((8,))]
        + [pltpu.VMEM((cubed, lx, ly, ez), BF), pltpu.VMEM((cubed, lx, ly, ez), BF),
           pltpu.VMEM((lx, ly, ez), jnp.int32), pltpu.VMEM(packed.shape, BF),
           pltpu.VMEM((cubed, el, ez), BF), pltpu.VMEM((cubed, el, ez), F32),
           pltpu.SemaphoreType.DMA, pltpu.SemaphoreType.DMA((n + 3,))],
        compiler_params=pltpu.CompilerParams(
            collective_id=0, has_side_effects=True, vmem_limit_bytes=48 << 20
        ),
        name="exchange",
    )(sol, src, degree, packed)
    updated, residual = pl.pallas_call(
        functools.partial(fine_kernel, n, slots),
        out_shape=[sd((cubed, lx, ly, ez), F32), sd((cubed, lx, ly, ez), BF)],
        in_specs=[vmem, hbm] + [vmem] * 6,
        out_specs=[hbm] * 2,
        scratch_shapes=[pltpu.VMEM((cubed, lx, ly, ez), F32), pltpu.VMEM((cubed, lx, ly, ez), BF),
                        pltpu.VMEM((cubed, el, ez), F32), pltpu.SemaphoreType.DMA((n,)),
                        pltpu.SemaphoreType.DMA((n,)), pltpu.SemaphoreType.DMA((n,))],
        compiler_params=pltpu.CompilerParams(vmem_limit_bytes=48 << 20),
        name="fine",
    )(*outs, degree, packed)
    return updated.reshape(solution.shape), residual.reshape(solution.shape)


def solution(mesh):
    spec = P(None, None, None, "mem", "grp", None)
    return jax.shard_map(
        per_device,
        mesh=mesh,
        in_specs=(spec, spec, P("mem", "grp", None)),
        out_specs=(spec, spec),
        check_vma=False,
    )
```
